32 devices in a mesh: block: 8 (over z, x), tok: 4 (over y, core).
Axes of the slice: x: 2, y: 2, z: 4, core: 2. Of those that a mesh axis runs over, the one named last changes fastest.
Arguments:
- fast_in: float32 [8, 4, 3, 512, 512], P('block', 'tok'), may hold values from -0.25 to 0.25
- queries: bfloat16 [3, 8, 512, 2048], P(None, 'block', 'tok'), may hold values from -6 to 6
- keys: bfloat16 [3, 8, 512, 2048], P(None, 'block', 'tok'), may hold values from -6 to 6
- values: bfloat16 [3, 8, 512, 2048], P(None, 'block', 'tok'), may hold values from -6 to 6
- rates: bfloat16 [3, 8, 512, 4], P(None, 'block', 'tok'), may hold values from 0.0009765625 to 0.0078125
Outputs:
- outputs: bfloat16 [3, 8, 512, 2048], P(None, 'block', 'tok')
- fast_out: float32 [8, 4, 3, 512, 512], P('block', 'tok')
The draws below stay inside these ranges and needn't reach their ends.
All inputs are finite; a program needn't handle non-finite values.
Results may differ from the reference program's by a relative error of at most 0.002.
Values may be sent and summed in bfloat16 or wider, within the bound.
A program may use at most 128 MiB of HBM per device.

```python
import math
import jax
import jax.numpy as jnp
from jax import lax

HEADS = 4
DH = 512
STEPS = 3
BLOCK = 512
OWNERS = 8
WIDTH = 2048


def level_of(rng, dims, split, low, high):
    gain, own = 1.0, jax.random.fold_in(rng, 6)
    for axis_at, blocks in split:
        steps = jnp.exp(jax.random.uniform(jax.random.fold_in(own, axis_at), (blocks,), jnp.float32, low / len(split), high / len(split)))
        gain = gain * jnp.repeat(steps, dims[axis_at] // blocks).reshape([-1 if axis == axis_at else 1 for axis in range(len(dims))])
    return gain


def scatter_about(own_key, dims, scale, reach, cuts=(), held_as=jnp.bfloat16):
    values = scale * jax.random.normal(own_key, dims, jnp.float32)
    if cuts:
        values = values * level_of(own_key, dims, cuts, -0.22, 0.18)
    return jnp.clip(values, -reach, reach).astype(held_as)


def setup_inputs(seed: int = 0) -> dict:
    arg_keys = jax.random.split(jax.random.key(seed), 6)
    fast_in = scatter_about(arg_keys[0], (OWNERS, HEADS, 3, DH, DH), DH ** -0.5, 0.25, ((0, 8), (1, 4)), jnp.float32)
    queries = scatter_about(arg_keys[1], (STEPS, OWNERS, BLOCK, WIDTH), 1.0, 6.0, ((1, 8), (2, 4)))
    keys = scatter_about(arg_keys[2], (STEPS, OWNERS, BLOCK, WIDTH), 1.0, 6.0, ((1, 8), (2, 4)))
    values = scatter_about(arg_keys[3], (STEPS, OWNERS, BLOCK, WIDTH), 1.0, 6.0, ((1, 8), (2, 4)))
    rates = jnp.clip(jnp.exp(math.log(0.0078125) - 2.0794415 * jax.random.uniform(arg_keys[4], (STEPS, OWNERS, BLOCK, HEADS), jnp.float32) ** level_of(arg_keys[4], (STEPS, OWNERS, BLOCK, HEADS), ((1, 8), (2, 4)), -0.2, 0.2)), 0.0009765625, 0.0078125).astype(jnp.bfloat16)
    return dict(fast_in=fast_in, queries=queries, keys=keys, values=values, rates=rates)


precise = lax.Precision.HIGHEST
epsilon = 1e-06

def renormed(initial, stepped):
    rescale = jnp.sqrt((lax.optimization_barrier(jnp.mean(initial * initial, axis=-1)) + epsilon) / (lax.optimization_barrier(jnp.mean(stepped * stepped, axis=-1)) + epsilon))
    return stepped * rescale[..., None]

def fast_update(weights, key_full, value_full, rate_full):
    hidden = jnp.einsum('thd,hdf->thf', key_full, weights[:, 0], precision=precise)
    gated = jnp.einsum('thd,hdf->thf', key_full, weights[:, 1], precision=precise)
    gate_sig = jax.nn.sigmoid(hidden)
    active = hidden * gate_sig
    target = -rate_full[:, :, None] * value_full
    grad_down = jnp.einsum('thf,the->hfe', active * gated, target, precision=precise)
    back_grad = jnp.einsum('the,hfe->thf', target, weights[:, 2], precision=precise)
    grad_first = jnp.einsum('thd,thf->hdf', key_full, back_grad * gated * gate_sig * (1.0 + hidden * (1.0 - gate_sig)), precision=precise)
    grad_gate = jnp.einsum('thd,thf->hdf', key_full, back_grad * active, precision=precise)
    new_down = renormed(weights[:, 2], weights[:, 2] - grad_down)
    new_inner = renormed(weights[:, :2], weights[:, :2] - jnp.stack([grad_first, grad_gate], axis=1))
    return jnp.concatenate([new_inner, new_down[:, None]], axis=1)

def apply_fast(updated, query_full):
    hidden = jnp.einsum('thd,hdf->thf', query_full, updated[:, 0], precision=precise)
    gated = jnp.einsum('thd,hdf->thf', query_full, updated[:, 1], precision=precise)
    return jnp.einsum('thf,hfe->the', jax.nn.silu(hidden) * gated, updated[:, 2], precision=precise)

def reference(fast_in, queries, keys, values, rates):
    head_count = fast_in.shape[1]
    head_width = fast_in.shape[3]
    block_len = queries.shape[2]
    current = fast_in
    results = []
    for round_index in range(STEPS):
        if round_index > 0:
            current = jnp.roll(current, 1, axis=0)

        def one_owner(packed):
            weights, query_now, key_now, value_now, rate_now = packed
            query_full = query_now.astype(jnp.float32).reshape(block_len, head_count, head_width)
            key_full = key_now.astype(jnp.float32).reshape(block_len, head_count, head_width)
            value_full = value_now.astype(jnp.float32).reshape(block_len, head_count, head_width)
            rate_full = rate_now.astype(jnp.float32)
            updated = fast_update(weights, key_full, value_full, rate_full)
            result = apply_fast(updated, query_full).reshape(block_len, head_count * head_width).astype(jnp.bfloat16)
            return (updated, result)
        current, result = lax.map(one_owner, (current, queries[round_index], keys[round_index], values[round_index], rates[round_index]))
        results.append(result)
    return (jnp.stack(results, axis=0), current)
```

```python
import functools
import math

import jax
import jax.numpy as jnp
from jax import lax
from jax.experimental import pallas as pl
from jax.experimental.pallas import tpu as pltpu
from jax.sharding import PartitionSpec as P

MESH = pl.DeviceIdType.MESH
epsilon = 1e-06
BF, F32 = jnp.bfloat16, jnp.float32
CHUNK = 256


def mm(a, b, dims=((1,), (0,))):
    return lax.dot_general(a, b, (dims, ((), ())), preferred_element_type=F32)


def split(x):
    hi = x.astype(BF)
    return hi, (x - hi.astype(F32)).astype(BF)


def encode(x):
    two = x * x
    return (two * two * two * x * jnp.abs(x)).astype(BF)


def decode(y):
    y = y.astype(F32)
    root = lax.rsqrt(lax.rsqrt(lax.rsqrt(jnp.maximum(jnp.abs(y), 2.0 ** -126))))
    two = root * root
    return y * (two * two * two * root)


def kernel(blocks, toks, scale, fast_ref, q_ref, k_ref, v_ref, rate_ref, out_ref, fast_out_ref,
           held, rate_wide, wf, whi, wlo, wsend, wrecv, abuf, xbuf, obuf, eta,
           recv_sem, send_sem, wload_sem, wsend_sem, wrecv_sem, orecv_sem, osend_sem):
    steps = q_ref.shape[0]
    part = q_ref.shape[2]
    width = wf.shape[1]
    length = held.shape[2]
    rows_of = min(CHUNK, width, length)
    b, t = lax.axis_index("block"), lax.axis_index("tok")
    after, before = lax.rem(b + 1, blocks), lax.rem(b + blocks - 1, blocks)
    after2, before2 = lax.rem(b + 2, blocks), lax.rem(b + blocks - 2, blocks)
    near = lax.div(t, 2) * 2
    mate = near + lax.rem(t + 1, 2)
    far = [lax.rem(near + 2 + j, toks) for j in range(2)]
    others = far + [mate]
    sources = (k_ref, v_ref, q_ref)

    def load_w(m):
        return pltpu.make_async_copy(fast_ref.at[0, 0, m], wf.at[m], wload_sem.at[m])

    for m in range(3):
        load_w(m).start()

    def src_of(s, a, dest):
        if a == 3:
            return rate_wide.at[s, dest]
        return sources[a].at[s, 0, :, pl.ds(pl.multiple_of(dest * width, width), width)]

    def dst_of(s, a, origin):
        rows = pl.ds(pl.multiple_of(origin * part, part), part)
        return eta.at[s, rows] if a == 3 else held.at[a, s, rows]

    def own(s, a):
        return pltpu.make_async_copy(src_of(s, a, t), dst_of(s, a, t), recv_sem.at[s, a, t])

    sends = []

    def send(s, a, block, dest, slot):
        copy = pltpu.make_async_remote_copy(
            src_ref=src_of(s, a, dest), dst_ref=dst_of(s, a, t),
            send_sem=send_sem.at[s, a, slot], recv_sem=recv_sem.at[s, a, t],
            device_id=(block, dest), device_id_type=MESH)
        copy.start()
        sends.append(copy)

    def exchange(s, a):
        for slot, dest in enumerate(others):
            send(s, a, b, dest, slot)

    def wait_tokens(s, a):
        for origin in range(toks):
            ref = dst_of(s, a, origin)
            pltpu.make_async_copy(ref, ref, recv_sem.at[s, a, origin]).wait()

    for a in (0, 1, 2):
        own(0, a).start()
        own(2, a).start()
    for s in range(steps):
        for h in range(toks):
            rate_wide[s, h] = jnp.broadcast_to(rate_ref[s, 0, :, h:h + 1], rate_wide.shape[2:])
    own(0, 3).start()
    own(2, 3).start()

    barrier = pltpu.get_barrier_semaphore()
    greet = [(b, dest) for dest in others]
    greet += [(block, tok) for block in (after, before) for tok in range(toks)]
    greet += [(after2, t), (before2, t)]
    for device in greet:
        pl.semaphore_signal(barrier, inc=1, device_id=device, device_id_type=MESH)
    pl.semaphore_wait(barrier, len(greet))

    for a in (0, 3, 1):
        exchange(0, a)
    for a in (0, 3, 1):
        for slot, dest in enumerate((near, near + 1)):
            send(1, a, after, dest, 2 + slot)

    def split_weights(m):
        @pl.loop(0, width // rows_of)
        def _(i):
            rows = pl.ds(pl.multiple_of(i * rows_of, rows_of), rows_of)
            whi[m, rows], wlo[m, rows] = split(wf[m, rows])

    for m in range(3):
        load_w(m).wait()
        split_weights(m)

    def forward(s):
        @pl.loop(0, length // rows_of)
        def _(i):
            rows = pl.ds(pl.multiple_of(i * rows_of, rows_of), rows_of)
            k, v = held[0, s, rows], held[1, s, rows]
            rate = eta[s, rows].astype(F32)
            rate = jnp.concatenate([rate] * (width // rate.shape[1]), axis=1)
            hidden = mm(k, whi[0]) + mm(k, wlo[0])
            gated = mm(k, whi[1]) + mm(k, wlo[1])
            gate_sig = jax.nn.sigmoid(hidden)
            active = hidden * gate_sig
            abuf[0, rows], abuf[1, rows] = split(rate * (active * gated))
            back = rate * (mm(v, whi[2], ((1,), (1,))) + mm(v, wlo[2], ((1,), (1,))))
            first = back * gated * gate_sig * (1.0 + hidden * (1.0 - gate_sig))
            xbuf[0, rows], xbuf[1, rows] = split(first)
            xbuf[2, rows], xbuf[3, rows] = split(back * active)

    def update(s, m, passing):
        @pl.loop(0, width // rows_of)
        def _(i):
            at = pl.multiple_of(i * rows_of, rows_of)
            rows = pl.ds(at, rows_of)
            over = ((0,), (0,))
            if m == 2:
                v = held[1, s]
                grad = mm(abuf[0, :, rows], v, over) + mm(abuf[1, :, rows], v, over)
            else:
                k = held[0, s, :, rows]
                grad = mm(k, xbuf[2 * m], over) + mm(k, xbuf[2 * m + 1], over)
            old = wf[m, rows]
            new = old + grad
            rescale = jnp.sqrt((jnp.mean(old * old, axis=1, keepdims=True) + epsilon)
                               / (jnp.mean(new * new, axis=1, keepdims=True) + epsilon))
            new = new * rescale
            wf[m, rows] = new
            whi[m, rows], wlo[m, rows] = split(new)
            if passing:
                wsend[m, rows] = encode(new * scale)

    def apply(s):
        @pl.loop(0, length // rows_of)
        def _(i):
            rows = pl.ds(pl.multiple_of(i * rows_of, rows_of), rows_of)
            q = held[2, s, rows]
            hidden = mm(q, whi[0]) + mm(q, wlo[0])
            gated = mm(q, whi[1]) + mm(q, wlo[1])
            hi, lo = split(jax.nn.silu(hidden) * gated)
            result = mm(hi, whi[2]) + (mm(lo, whi[2]) + mm(hi, wlo[2]))
            obuf[s, rows] = result.astype(BF)

    def out_at(s, origin):
        return out_ref.at[s, 0, :, pl.ds(pl.multiple_of(origin * width, width), width)]

    def out_part(s, dest):
        return obuf.at[s, pl.ds(pl.multiple_of(dest * part, part), part)]

    def send_out(s, block, dests):
        for slot, dest in enumerate(dests):
            copy = pltpu.make_async_remote_copy(
                src_ref=out_part(s, dest), dst_ref=out_at(s, t),
                send_sem=osend_sem.at[s, slot], recv_sem=orecv_sem.at[s, t],
                device_id=(block, dest), device_id_type=MESH)
            copy.start()
            sends.append(copy)

    def own_out(s):
        pltpu.make_async_copy(out_part(s, t), out_at(s, t), orecv_sem.at[s, t]).start()

    def hand_on(m):
        return pltpu.make_async_remote_copy(
            src_ref=wsend.at[m], dst_ref=wrecv.at[m], send_sem=wsend_sem.at[m],
            recv_sem=wrecv_sem.at[m], device_id=(after2, t), device_id_type=MESH)

    for a in (0, 3, 1):
        wait_tokens(0, a)
    for a in (0, 3, 1):
        for slot, dest in enumerate(far):
            send(1, a, after, dest, slot)
    forward(0)
    for m in (2, 0, 1):
        update(0, m, True)
        hand_on(m).start()
    exchange(0, 2)
    for a in (0, 3, 1, 2):
        exchange(2, a)
    wait_tokens(0, 2)
    apply(0)
    send_out(0, b, others)
    own_out(0)

    for m in (2, 0, 1):
        hand_on(m).wait()
        if m == 1:
            for slot, dest in enumerate(far + [near, near + 1]):
                send(1, 2, after, dest, slot)

        @pl.loop(0, width // rows_of)
        def _(i):
            rows = pl.ds(pl.multiple_of(i * rows_of, rows_of), rows_of)
            fresh = decode(wrecv[m, rows]) * (1.0 / scale)
            wf[m, rows] = fresh
            whi[m, rows], wlo[m, rows] = split(fresh)
    for a in (0, 3, 1):
        wait_tokens(1, a)
    forward(1)
    for m in (2, 0, 1):
        update(1, m, False)
    wait_tokens(1, 2)
    apply(1)
    send_out(1, before, far + [near, near + 1])

    for a in (0, 3, 1):
        wait_tokens(2, a)
    forward(2)
    for m in (2, 0, 1):
        update(2, m, False)
        pltpu.make_async_copy(wf.at[m], fast_out_ref.at[0, 0, m], wload_sem.at[m]).start()
    wait_tokens(2, 2)
    apply(2)
    send_out(2, b, others)
    own_out(2)

    for s in range(steps):
        for origin in range(toks):
            ref = out_at(s, origin)
            pltpu.make_async_copy(ref, ref, orecv_sem.at[s, origin]).wait()
    for m in range(3):
        pltpu.make_async_copy(wf.at[m], fast_out_ref.at[0, 0, m], wload_sem.at[m]).wait()
    for copy in sends:
        copy.wait_send()


def local(fast_in, queries, keys, values, rates):
    blocks, toks = lax.axis_size("block"), lax.axis_size("tok")
    steps, _, part, _ = queries.shape
    width = fast_in.shape[-1]
    length = part * toks
    scale = 2.0 ** math.floor(math.log2(2.0 ** 15.8 / (0.2501 * math.sqrt(width))))
    anywhere = pl.BlockSpec(memory_space=pl.ANY)
    vmem, dma = pltpu.VMEM, pltpu.SemaphoreType.DMA
    lanes = 128
    return pl.pallas_call(
        functools.partial(kernel, blocks, toks, scale),
        out_shape=(jax.ShapeDtypeStruct(queries.shape, queries.dtype),
                   jax.ShapeDtypeStruct(fast_in.shape, fast_in.dtype)),
        in_specs=[anywhere] * 4 + [pl.BlockSpec(memory_space=pltpu.VMEM)],
        out_specs=(anywhere, anywhere),
        scratch_shapes=[
            vmem((3, steps, length, width), BF),
            vmem((steps, toks, part, lanes), BF),
            vmem((3, width, width), F32),
            vmem((3, width, width), BF),
            vmem((3, width, width), BF),
            vmem((3, width, width), BF),
            vmem((3, width, width), BF),
            vmem((2, length, width), BF),
            vmem((4, length, width), BF),
            vmem((steps, length, width), BF),
            vmem((steps, length, lanes), BF),
            dma((steps, 4, toks)), dma((steps, 4, toks)),
            dma((3,)), dma((3,)), dma((3,)),
            dma((steps, toks)), dma((steps, toks)),
        ],
        compiler_params=pltpu.CompilerParams(
            collective_id=0, has_side_effects=True, vmem_limit_bytes=48 * 2**20),
        cost_estimate=pl.CostEstimate(
            flops=57 * 2 * length * width * width, bytes_accessed=2**24, transcendentals=0),
    )(fast_in, queries, keys, values, rates)


def solution(mesh):
    tokens = P(None, "block", "tok", None)
    weights = P("block", "tok", None, None, None)
    return jax.shard_map(
        local, mesh=mesh, in_specs=(weights, tokens, tokens, tokens, tokens),
        out_specs=(tokens, weights), check_vma=False)
```

```python
import functools
import math

import jax
import jax.numpy as jnp
from jax import lax
from jax.experimental import pallas as pl
from jax.experimental.pallas import tpu as pltpu
from jax.sharding import PartitionSpec as P

MESH = pl.DeviceIdType.MESH
epsilon = 1e-06
BF, F32 = jnp.bfloat16, jnp.float32
CHUNK = 256


def mm(a, b, dims=((1,), (0,))):
    return lax.dot_general(a, b, (dims, ((), ())), preferred_element_type=F32)


def split(x):
    hi = x.astype(BF)
    return hi, (x - hi.astype(F32)).astype(BF)


def encode(x):
    two = x * x
    return (two * two * two * x * jnp.abs(x)).astype(BF)


def decode(y):
    y = y.astype(F32)
    root = lax.rsqrt(lax.rsqrt(lax.rsqrt(jnp.maximum(jnp.abs(y), 2.0 ** -126))))
    two = root * root
    return y * (two * two * two * root)


def kernel(blocks, toks, scale, fast_ref, q_ref, k_ref, v_ref, rate_ref, out_ref, fast_out_ref,
           held, rate_wide, wf, whi, wlo, wsend, wrecv, abuf, fbuf, xbuf, obuf, eta,
           recv_sem, send_sem, wload_sem, wsend_sem, wrecv_sem, orecv_sem, osend_sem):
    steps = q_ref.shape[0]
    part = q_ref.shape[2]
    width = wf.shape[1]
    length = held.shape[2]
    rows_of = min(CHUNK, width, length)
    b, t = lax.axis_index("block"), lax.axis_index("tok")
    odd = lax.rem(b, 2)
    pair = b + 1 - 2 * odd
    after2, before2 = lax.rem(b + 2, blocks), lax.rem(b + blocks - 2, blocks)
    near = lax.div(t, 2) * 2
    mate = near + lax.rem(t + 1, 2)
    far = [lax.rem(near + 2 + j, toks) for j in range(2)]
    side = [near, near + 1]
    others = far + [mate]
    sources = (k_ref, v_ref, q_ref)
    K, V, Q, RATE = range(4)

    def load_w(m):
        return pltpu.make_async_copy(fast_ref.at[0, 0, m], wf.at[m], wload_sem.at[m])

    for m in range(3):
        load_w(m).start()

    def src_of(s, a, dest):
        if a == RATE:
            return rate_wide.at[s, dest]
        return sources[a].at[s, 0, :, pl.ds(pl.multiple_of(dest * width, width), width)]

    def dst_of(s, a, origin):
        rows = pl.ds(pl.multiple_of(origin * part, part), part)
        return eta.at[s, rows] if a == RATE else held.at[a, s, rows]

    def own(s, a):
        return pltpu.make_async_copy(src_of(s, a, t), dst_of(s, a, t), recv_sem.at[s, a, t])

    sends = []

    def send(s, a, block, dest, slot):
        copy = pltpu.make_async_remote_copy(
            src_ref=src_of(s, a, dest), dst_ref=dst_of(s, a, t),
            send_sem=send_sem.at[s, a, slot], recv_sem=recv_sem.at[s, a, t],
            device_id=(block, dest), device_id_type=MESH)
        copy.start()
        sends.append(copy)

    def exchange(s, a):
        for slot, dest in enumerate(others):
            send(s, a, b, dest, slot)

    def wait_tokens(s, *arrays):
        for a in arrays:
            for origin in range(toks):
                ref = dst_of(s, a, origin)
                pltpu.make_async_copy(ref, ref, recv_sem.at[s, a, origin]).wait()

    for a in (K, V, Q):
        own(0, a).start()
        own(2, a).start()
    for s in range(steps):
        for h in range(toks):
            rate_wide[s, h] = jnp.broadcast_to(rate_ref[s, 0, :, h:h + 1], rate_wide.shape[2:])
    own(0, RATE).start()
    own(2, RATE).start()

    barrier = pltpu.get_barrier_semaphore()
    greet = [(b, dest) for dest in others] + [(pair, tok) for tok in range(toks)]
    greet += [(after2, t), (before2, t)]
    for device in greet:
        pl.semaphore_signal(barrier, inc=1, device_id=device, device_id_type=MESH)
    pl.semaphore_wait(barrier, len(greet))

    for a in (K, RATE, V):
        exchange(0, a)
    for a in (K, RATE, V):
        for slot, dest in enumerate(side):
            send(1, a, pair, dest, 2 + slot)

    def each(count):
        return pl.loop(0, count // rows_of)

    def chunk(i):
        return pl.ds(pl.multiple_of(i * rows_of, rows_of), rows_of)

    for m in range(3):
        load_w(m).wait()

        @each(width)
        def _(i):
            rows = chunk(i)
            whi[0, m, rows], wlo[0, m, rows] = split(wf[m, rows])

    def forward(s, bank):
        @each(length)
        def _(i):
            rows = chunk(i)
            k = held[K, s, rows]
            rate = eta[s, rows].astype(F32)
            rate = jnp.concatenate([rate] * (width // rate.shape[1]), axis=1)
            hidden = mm(k, whi[bank, 0]) + mm(k, wlo[bank, 0])
            gated = mm(k, whi[bank, 1]) + mm(k, wlo[bank, 1])
            gate_sig = jax.nn.sigmoid(hidden)
            active = rate * (hidden * gate_sig)
            abuf[0, rows], abuf[1, rows] = split(active * gated)
            fbuf[0, rows] = rate * gated * gate_sig * (1.0 + hidden * (1.0 - gate_sig))
            fbuf[1, rows] = active

    def backward(s, bank):
        @each(length)
        def _(i):
            rows = chunk(i)
            v = held[V, s, rows]
            over = ((1,), (1,))
            back = mm(v, whi[bank, 2], over) + mm(v, wlo[bank, 2], over)
            xbuf[0, rows], xbuf[1, rows] = split(back * fbuf[0, rows])
            xbuf[2, rows], xbuf[3, rows] = split(back * fbuf[1, rows])

    def update(s, m, bank):
        @each(width)
        def _(i):
            rows = chunk(i)
            over = ((0,), (0,))
            if m == 2:
                v = held[V, s]
                grad = mm(abuf[0, :, rows], v, over) + mm(abuf[1, :, rows], v, over)
            else:
                k = held[K, s, :, rows]
                grad = mm(k, xbuf[2 * m], over) + mm(k, xbuf[2 * m + 1], over)
            old = wf[m, rows]
            new = old + grad
            rescale = jnp.sqrt((jnp.mean(old * old, axis=1, keepdims=True) + epsilon)
                               / (jnp.mean(new * new, axis=1, keepdims=True) + epsilon))
            new = new * rescale
            wf[m, rows] = new
            whi[bank, m, rows], wlo[bank, m, rows] = split(new)

    def hand_on(m):
        return pltpu.make_async_remote_copy(
            src_ref=wsend.at[m], dst_ref=wrecv.at[m], send_sem=wsend_sem.at[m],
            recv_sem=wrecv_sem.at[m], device_id=(after2, t), device_id_type=MESH)

    def give(m):
        @each(width)
        def _(i):
            rows = chunk(i)
            wsend[m, rows] = encode(wf[m, rows] * scale)

        hand_on(m).start()

    def take(m, bank):
        hand_on(m).wait_recv()

        @each(width)
        def _(i):
            rows = chunk(i)
            fresh = decode(wrecv[m, rows]) * (1.0 / scale)
            wf[m, rows] = fresh
            whi[bank, m, rows], wlo[bank, m, rows] = split(fresh)

    def out_at(s, origin):
        return out_ref.at[s, 0, :, pl.ds(pl.multiple_of(origin * width, width), width)]

    def out_part(s, dest):
        return obuf.at[s, pl.ds(pl.multiple_of(dest * part, part), part)]

    def out_copy(s, block, dest, slot):
        return pltpu.make_async_remote_copy(
            src_ref=out_part(s, dest), dst_ref=out_at(s, t),
            send_sem=osend_sem.at[s, slot], recv_sem=orecv_sem.at[s, t],
            device_id=(block, dest), device_id_type=MESH)

    def apply(s, bank):
        wait_tokens(s, Q)
        home = s != 1
        block = b if home else pair
        for turn, dests in enumerate((far, side)):
            rows = pl.ds(pl.multiple_of(dests[0] * part, 2 * part), 2 * part)
            q = held[Q, s, rows]
            hidden = mm(q, whi[bank, 0]) + mm(q, wlo[bank, 0])
            gated = mm(q, whi[bank, 1]) + mm(q, wlo[bank, 1])
            hi, lo = split(jax.nn.silu(hidden) * gated)
            result = mm(hi, whi[bank, 2]) + (mm(lo, whi[bank, 2]) + mm(hi, wlo[bank, 2]))
            obuf[s, rows] = result.astype(BF)
            if turn and home:
                dests = [mate]
                pltpu.make_async_copy(out_part(s, t), out_at(s, t), orecv_sem.at[s, t]).start()
            for slot, dest in enumerate(dests):
                out_copy(s, block, dest, 2 * turn + slot).start()

    def wait_out_sent(s):
        home = s != 1
        block = b if home else pair
        for slot, dest in enumerate(others if home else far + side):
            out_copy(s, block, dest, slot).wait_send()

    wait_tokens(0, K, RATE)
    forward(0, 0)
    wait_tokens(0, V)
    for a in (K, RATE, V):
        for slot, dest in enumerate(far):
            send(1, a, pair, dest, slot)
    backward(0, 0)
    for m in range(3):
        update(0, m, 1)

        @pl.when(odd == 1)
        def _():
            give(m)

    exchange(0, Q)
    for slot, dest in enumerate(far + side):
        send(1, Q, pair, dest, slot)
    for a in (K, RATE, V, Q):
        exchange(2, a)

    @pl.when(odd == 0)
    def _():
        wait_tokens(1, K, RATE)
        forward(1, 1)
        wait_tokens(1, V)
        backward(1, 1)
        for m in range(3):
            update(1, m, 3)
            give(m)

    apply(0, 1)

    @pl.when(odd == 0)
    def _():
        apply(1, 3)
        take(0, 2)
        take(1, 2)
        wait_tokens(2, K, RATE)
        forward(2, 2)
        take(2, 2)
        wait_tokens(2, V)
        backward(2, 2)

    @pl.when(odd == 1)
    def _():
        take(0, 2)
        take(1, 2)
        wait_tokens(1, K, RATE)
        forward(1, 2)
        take(2, 2)
        wait_tokens(1, V)
        backward(1, 2)
        for m in range(3):
            update(1, m, 3)
        apply(1, 3)
        wait_tokens(2, K, RATE)
        forward(2, 3)
        wait_tokens(2, V)
        backward(2, 3)

    for m in range(3):
        update(2, m, 0)
        pltpu.make_async_copy(wf.at[m], fast_out_ref.at[0, 0, m], wload_sem.at[m]).start()
    apply(2, 0)

    for s in range(steps):
        for origin in range(toks):
            ref = out_at(s, origin)
            pltpu.make_async_copy(ref, ref, orecv_sem.at[s, origin]).wait()
        wait_out_sent(s)
    for m in range(3):
        pltpu.make_async_copy(wf.at[m], fast_out_ref.at[0, 0, m], wload_sem.at[m]).wait()
        hand_on(m).wait_send()
    for copy in sends:
        copy.wait_send()


def local(fast_in, queries, keys, values, rates):
    blocks, toks = lax.axis_size("block"), lax.axis_size("tok")
    steps, _, part, _ = queries.shape
    width = fast_in.shape[-1]
    length = part * toks
    scale = 2.0 ** math.floor(math.log2(2.0 ** 15.8 / (0.2501 * math.sqrt(width))))
    anywhere = pl.BlockSpec(memory_space=pl.ANY)
    vmem, dma = pltpu.VMEM, pltpu.SemaphoreType.DMA
    lanes = 128
    return pl.pallas_call(
        functools.partial(kernel, blocks, toks, scale),
        out_shape=(jax.ShapeDtypeStruct(queries.shape, queries.dtype),
                   jax.ShapeDtypeStruct(fast_in.shape, fast_in.dtype)),
        in_specs=[anywhere] * 4 + [pl.BlockSpec(memory_space=pltpu.VMEM)],
        out_specs=(anywhere, anywhere),
        scratch_shapes=[
            vmem((3, steps, length, width), BF),
            vmem((steps, toks, part, lanes), BF),
            vmem((3, width, width), F32),
            vmem((4, 3, width, width), BF),
            vmem((4, 3, width, width), BF),
            vmem((3, width, width), BF),
            vmem((3, width, width), BF),
            vmem((2, length, width), BF),
            vmem((2, length, width), F32),
            vmem((4, length, width), BF),
            vmem((steps, length, width), BF),
            vmem((steps, length, lanes), BF),
            dma((steps, 4, toks)), dma((steps, 4, toks)),
            dma((3,)), dma((3,)), dma((3,)),
            dma((steps, toks)), dma((steps, toks)),
        ],
        compiler_params=pltpu.CompilerParams(
            collective_id=0, has_side_effects=True, vmem_limit_bytes=60 * 2**20),
        cost_estimate=pl.CostEstimate(
            flops=57 * 2 * length * width * width, bytes_accessed=2**24, transcendentals=0),
    )(fast_in, queries, keys, values, rates)


def solution(mesh):
    tokens = P(None, "block", "tok", None)
    weights = P("block", "tok", None, None, None)
    return jax.shard_map(
        local, mesh=mesh, in_specs=(weights, tokens, tokens, tokens, tokens),
        out_specs=(tokens, weights), check_vma=False)
```

```python
import functools
import math

import jax
import jax.numpy as jnp
from jax import lax
from jax.experimental import pallas as pl
from jax.experimental.pallas import tpu as pltpu
from jax.sharding import PartitionSpec as P

MESH = pl.DeviceIdType.MESH
epsilon = 1e-06
BF, F32 = jnp.bfloat16, jnp.float32
CHUNK = 256


def mm(a, b, dims=((1,), (0,))):
    return lax.dot_general(a, b, (dims, ((), ())), preferred_element_type=F32)


def split(x):
    hi = x.astype(BF)
    return hi, (x - hi.astype(F32)).astype(BF)


def encode(x):
    two = x * x
    return (two * two * two * x * jnp.abs(x)).astype(BF)


def decode(y):
    y = y.astype(F32)
    root = lax.rsqrt(lax.rsqrt(lax.rsqrt(jnp.maximum(jnp.abs(y), 2.0 ** -126))))
    two = root * root
    return y * (two * two * two * root)


def kernel(blocks, toks, scale, fast_ref, q_ref, k_ref, v_ref, rate_ref, out_ref, fast_out_ref,
           held, rate_wide, wf, whi, wlo, wsend, wrecv, abuf, fbuf, xbuf, obuf, eta,
           recv_sem, send_sem, wload_sem, wsend_sem, wrecv_sem, orecv_sem, osend_sem):
    steps = q_ref.shape[0]
    part = q_ref.shape[2]
    width = wf.shape[1]
    length = held.shape[2]
    rows_of = min(CHUNK, width, length)
    b, t = lax.axis_index("block"), lax.axis_index("tok")
    odd = lax.rem(b, 2)
    pair = b + 1 - 2 * odd
    after2, before2 = lax.rem(b + 2, blocks), lax.rem(b + blocks - 2, blocks)
    near = lax.div(t, 2) * 2
    mate = near + lax.rem(t + 1, 2)
    far = [lax.rem(near + 2 + j, toks) for j in range(2)]
    side = [near, near + 1]
    others = far + [mate]
    sources = (k_ref, v_ref, q_ref)
    K, V, Q, RATE = range(4)

    def load_w(m):
        return pltpu.make_async_copy(fast_ref.at[0, 0, m], wf.at[m], wload_sem.at[m])

    for m in range(3):
        load_w(m).start()

    def src_of(s, a, dest):
        if a == RATE:
            return rate_wide.at[s, dest]
        return sources[a].at[s, 0, :, pl.ds(pl.multiple_of(dest * width, width), width)]

    def dst_of(s, a, origin):
        rows = pl.ds(pl.multiple_of(origin * part, part), part)
        return eta.at[s, rows] if a == RATE else held.at[a, s, rows]

    def own(s, a):
        return pltpu.make_async_copy(src_of(s, a, t), dst_of(s, a, t), recv_sem.at[s, a, t])

    def token_copy(s, a, block, dest, slot):
        return pltpu.make_async_remote_copy(
            src_ref=src_of(s, a, dest), dst_ref=dst_of(s, a, t),
            send_sem=send_sem.at[s, a, slot], recv_sem=recv_sem.at[s, a, t],
            device_id=(block, dest), device_id_type=MESH)

    def send(s, a, block, dest, slot):
        token_copy(s, a, block, dest, slot).start()

    def exchange(s, a):
        for slot, dest in enumerate(others):
            send(s, a, b, dest, slot)

    def wait_tokens(s, *arrays):
        for a in arrays:
            for origin in range(toks):
                ref = dst_of(s, a, origin)
                pltpu.make_async_copy(ref, ref, recv_sem.at[s, a, origin]).wait()

    for a in (K, V, Q):
        own(0, a).start()
        own(2, a).start()

    def widen(s):
        rate = rate_ref[s, 0].astype(F32)
        for h in range(toks):
            wide = jnp.broadcast_to(rate[h:h + 1], (rate_wide.shape[3], part))
            rate_wide[s, h] = wide.T.astype(BF)

    widen(0)
    own(0, RATE).start()

    barrier = pltpu.get_barrier_semaphore()
    greet = [(b, dest) for dest in others] + [(pair, tok) for tok in range(toks)]
    greet += [(after2, t), (before2, t)]
    for device in greet:
        pl.semaphore_signal(barrier, inc=1, device_id=device, device_id_type=MESH)
    pl.semaphore_wait(barrier, len(greet))

    for a in (K, RATE, V):
        exchange(0, a)
    widen(1)
    for a in (K, RATE, V):
        for slot, dest in enumerate(side):
            send(1, a, pair, dest, 2 + slot)
    widen(2)
    own(2, RATE).start()

    def each(count):
        return pl.loop(0, count // rows_of)

    def chunk(i):
        return pl.ds(pl.multiple_of(i * rows_of, rows_of), rows_of)

    for m in range(3):
        load_w(m).wait()

        @each(width)
        def _(i):
            rows = chunk(i)
            whi[0, m, rows], wlo[0, m, rows] = split(wf[m, rows])

    def forward(s, bank):
        @each(length)
        def _(i):
            rows = chunk(i)
            k = held[K, s, rows]
            rate = eta[s, rows].astype(F32)
            rate = jnp.concatenate([rate] * (width // rate.shape[1]), axis=1)
            hidden = mm(k, whi[bank, 0]) + mm(k, wlo[bank, 0])
            gated = mm(k, whi[bank, 1]) + mm(k, wlo[bank, 1])
            gate_sig = jax.nn.sigmoid(hidden)
            active = rate * (hidden * gate_sig)
            abuf[0, rows], abuf[1, rows] = split(active * gated)
            fbuf[0, rows] = rate * gated * gate_sig * (1.0 + hidden * (1.0 - gate_sig))
            fbuf[1, rows] = active

    def backward(s, bank):
        @each(length)
        def _(i):
            rows = chunk(i)
            v = held[V, s, rows]
            over = ((1,), (1,))
            back = mm(v, whi[bank, 2], over) + mm(v, wlo[bank, 2], over)
            xbuf[0, rows], xbuf[1, rows] = split(back * fbuf[0, rows])
            xbuf[2, rows], xbuf[3, rows] = split(back * fbuf[1, rows])

    def update(s, m, bank):
        @each(width)
        def _(i):
            rows = chunk(i)
            over = ((0,), (0,))
            if m == 2:
                v = held[V, s]
                grad = mm(abuf[0, :, rows], v, over) + mm(abuf[1, :, rows], v, over)
            else:
                k = held[K, s, :, rows]
                grad = mm(k, xbuf[2 * m], over) + mm(k, xbuf[2 * m + 1], over)
            old = wf[m, rows]
            new = old + grad
            rescale = jnp.sqrt((jnp.mean(old * old, axis=1, keepdims=True) + epsilon)
                               / (jnp.mean(new * new, axis=1, keepdims=True) + epsilon))
            new = new * rescale
            wf[m, rows] = new
            whi[bank, m, rows], wlo[bank, m, rows] = split(new)

    def hand_on(m):
        return pltpu.make_async_remote_copy(
            src_ref=wsend.at[m], dst_ref=wrecv.at[m], send_sem=wsend_sem.at[m],
            recv_sem=wrecv_sem.at[m], device_id=(after2, t), device_id_type=MESH)

    def give(m):
        @each(width)
        def _(i):
            rows = chunk(i)
            wsend[m, rows] = encode(wf[m, rows] * scale)

        hand_on(m).start()

    def take(m, bank):
        hand_on(m).wait_recv()

        @each(width)
        def _(i):
            rows = chunk(i)
            fresh = decode(wrecv[m, rows]) * (1.0 / scale)
            wf[m, rows] = fresh
            whi[bank, m, rows], wlo[bank, m, rows] = split(fresh)

    def out_at(s, origin):
        return out_ref.at[s, 0, :, pl.ds(pl.multiple_of(origin * width, width), width)]

    def out_part(s, dest):
        return obuf.at[s, pl.ds(pl.multiple_of(dest * part, part), part)]

    def out_copy(s, block, dest, slot):
        return pltpu.make_async_remote_copy(
            src_ref=out_part(s, dest), dst_ref=out_at(s, t),
            send_sem=osend_sem.at[s, slot], recv_sem=orecv_sem.at[s, t],
            device_id=(block, dest), device_id_type=MESH)

    def apply(s, bank):
        wait_tokens(s, Q)
        home = s != 1
        block = b if home else pair
        for turn, dests in enumerate((far, side)):
            rows = pl.ds(pl.multiple_of(dests[0] * part, 2 * part), 2 * part)
            q = held[Q, s, rows]
            hidden = mm(q, whi[bank, 0]) + mm(q, wlo[bank, 0])
            gated = mm(q, whi[bank, 1]) + mm(q, wlo[bank, 1])
            hi, lo = split(jax.nn.silu(hidden) * gated)
            result = mm(hi, whi[bank, 2]) + (mm(lo, whi[bank, 2]) + mm(hi, wlo[bank, 2]))
            obuf[s, rows] = result.astype(BF)
            if turn and home:
                dests = [mate]
                pltpu.make_async_copy(out_part(s, t), out_at(s, t), orecv_sem.at[s, t]).start()
            for slot, dest in enumerate(dests):
                out_copy(s, block, dest, 2 * turn + slot).start()

    def wait_out_sent(s):
        home = s != 1
        block = b if home else pair
        for slot, dest in enumerate(others if home else far + side):
            out_copy(s, block, dest, slot).wait_send()

    wait_tokens(0, K, RATE)
    forward(0, 0)
    wait_tokens(0, V)
    for a in (K, RATE, V):
        for slot, dest in enumerate(far):
            send(1, a, pair, dest, slot)
    backward(0, 0)
    for m in range(3):
        update(0, m, 1)

        @pl.when(odd == 1)
        def _():
            give(m)

    def send_rest():
        exchange(0, Q)
        for slot, dest in enumerate(far + side):
            send(1, Q, pair, dest, slot)
        for a in (K, RATE, V, Q):
            exchange(2, a)

    @pl.when(odd == 1)
    def _():
        wait_tokens(1, K, RATE, V)
        send_rest()

    @pl.when(odd == 0)
    def _():
        wait_tokens(1, K, RATE)
        forward(1, 1)
        wait_tokens(1, V)
        send_rest()
        backward(1, 1)
        for m in range(3):
            update(1, m, 3)
            give(m)

    apply(0, 1)

    @pl.when(odd == 0)
    def _():
        apply(1, 3)
        take(0, 2)
        take(1, 2)
        wait_tokens(2, K, RATE)
        forward(2, 2)
        take(2, 2)
        wait_tokens(2, V)
        backward(2, 2)

    @pl.when(odd == 1)
    def _():
        take(0, 2)
        take(1, 2)
        forward(1, 2)
        take(2, 2)
        backward(1, 2)
        for m in range(3):
            update(1, m, 3)
        apply(1, 3)
        wait_tokens(2, K, RATE)
        forward(2, 3)
        wait_tokens(2, V)
        backward(2, 3)

    for m in range(3):
        update(2, m, 0)
        pltpu.make_async_copy(wf.at[m], fast_out_ref.at[0, 0, m], wload_sem.at[m]).start()
    apply(2, 0)

    for s in range(steps):
        for origin in range(toks):
            ref = out_at(s, origin)
            pltpu.make_async_copy(ref, ref, orecv_sem.at[s, origin]).wait()
        wait_out_sent(s)
    for m in range(3):
        pltpu.make_async_copy(wf.at[m], fast_out_ref.at[0, 0, m], wload_sem.at[m]).wait()
        hand_on(m).wait_send()
    for a in range(4):
        for s in (0, 2):
            for slot, dest in enumerate(others):
                token_copy(s, a, b, dest, slot).wait_send()
        for slot, dest in enumerate(far + side):
            token_copy(1, a, pair, dest, slot).wait_send()


def local(fast_in, queries, keys, values, rates):
    blocks, toks = lax.axis_size("block"), lax.axis_size("tok")
    steps, _, part, _ = queries.shape
    width = fast_in.shape[-1]
    length = part * toks
    scale = 2.0 ** math.floor(math.log2(2.0 ** 15.8 / (0.2501 * math.sqrt(width))))
    anywhere = pl.BlockSpec(memory_space=pl.ANY)
    vmem, dma = pltpu.VMEM, pltpu.SemaphoreType.DMA
    lanes = 128
    return pl.pallas_call(
        functools.partial(kernel, blocks, toks, scale),
        out_shape=(jax.ShapeDtypeStruct(queries.shape, queries.dtype),
                   jax.ShapeDtypeStruct(fast_in.shape, fast_in.dtype)),
        in_specs=[anywhere] * 4 + [pl.BlockSpec(memory_space=pltpu.VMEM)],
        out_specs=(anywhere, anywhere),
        scratch_shapes=[
            vmem((3, steps, length, width), BF),
            vmem((steps, toks, part, lanes), BF),
            vmem((3, width, width), F32),
            vmem((4, 3, width, width), BF),
            vmem((4, 3, width, width), BF),
            vmem((3, width, width), BF),
            vmem((3, width, width), BF),
            vmem((2, length, width), BF),
            vmem((2, length, width), F32),
            vmem((4, length, width), BF),
            vmem((steps, length, width), BF),
            vmem((steps, length, lanes), BF),
            dma((steps, 4, toks)), dma((steps, 4, toks)),
            dma((3,)), dma((3,)), dma((3,)),
            dma((steps, toks)), dma((steps, toks)),
        ],
        compiler_params=pltpu.CompilerParams(
            collective_id=0, has_side_effects=True, vmem_limit_bytes=60 * 2**20),
        cost_estimate=pl.CostEstimate(
            flops=57 * 2 * length * width * width, bytes_accessed=2**24, transcendentals=0),
    )(fast_in, queries, keys, values, jnp.swapaxes(rates, 2, 3))


def solution(mesh):
    tokens = P(None, "block", "tok", None)
    weights = P("block", "tok", None, None, None)
    return jax.shard_map(
        local, mesh=mesh, in_specs=(weights, tokens, tokens, tokens, tokens),
        out_specs=(tokens, weights), check_vma=False)
```

```python
import functools
import math

import jax
import jax.numpy as jnp
from jax import lax
from jax.experimental import pallas as pl
from jax.experimental.pallas import tpu as pltpu
from jax.sharding import PartitionSpec as P

MESH = pl.DeviceIdType.MESH
epsilon = 1e-06
BF, F32 = jnp.bfloat16, jnp.float32
CHUNK = 256


def mm(a, b, dims=((1,), (0,))):
    return lax.dot_general(a, b, (dims, ((), ())), preferred_element_type=F32)


def split(x):
    hi = x.astype(BF)
    return hi, (x - hi.astype(F32)).astype(BF)


def encode(x):
    two = x * x
    return (two * two * two * x * jnp.abs(x)).astype(BF)


def decode(y):
    y = y.astype(F32)
    root = lax.rsqrt(lax.rsqrt(lax.rsqrt(jnp.maximum(jnp.abs(y), 2.0 ** -126))))
    two = root * root
    return y * (two * two * two * root)


def kernel(blocks, toks, scale, fast_ref, q_ref, k_ref, v_ref, rate_ref, out_ref, fast_out_ref,
           held, rate_wide, wf, whi, wlo, wsend, wrecv, abuf, fbuf, xbuf, obuf, eta,
           recv_sem, send_sem, wload_sem, wsend_sem, wrecv_sem, orecv_sem, osend_sem):
    steps = q_ref.shape[0]
    part = q_ref.shape[2]
    width = wf.shape[1]
    length = held.shape[2]
    rows_of = min(CHUNK, width, length)
    b, t = lax.axis_index("block"), lax.axis_index("tok")
    odd = lax.rem(b, 2)
    pair = b + 1 - 2 * odd
    after2, before2 = lax.rem(b + 2, blocks), lax.rem(b + blocks - 2, blocks)
    near = lax.div(t, 2) * 2
    mate = near + lax.rem(t + 1, 2)
    far = [lax.rem(near + 2 + j, toks) for j in range(2)]
    side = [near, near + 1]
    others = far + [mate]
    sources = (k_ref, v_ref, q_ref)
    K, V, Q, RATE = range(4)

    def load_w(m):
        return pltpu.make_async_copy(fast_ref.at[0, 0, m], wf.at[m], wload_sem.at[m])

    for m in range(3):
        load_w(m).start()

    def src_of(s, a, dest):
        if a == RATE:
            return rate_wide.at[s, dest]
        return sources[a].at[s, 0, :, pl.ds(pl.multiple_of(dest * width, width), width)]

    def dst_of(s, a, origin):
        rows = pl.ds(pl.multiple_of(origin * part, part), part)
        return eta.at[s, rows] if a == RATE else held.at[a, s, rows]

    def own(s, a):
        return pltpu.make_async_copy(src_of(s, a, t), dst_of(s, a, t), recv_sem.at[s, a, t])

    def token_copy(s, a, block, dest, slot):
        return pltpu.make_async_remote_copy(
            src_ref=src_of(s, a, dest), dst_ref=dst_of(s, a, t),
            send_sem=send_sem.at[s, a, slot], recv_sem=recv_sem.at[s, a, t],
            device_id=(block, dest), device_id_type=MESH)

    def send(s, a, block, dest, slot):
        token_copy(s, a, block, dest, slot).start()

    def exchange(s, a):
        for slot, dest in enumerate(others):
            send(s, a, b, dest, slot)

    def wait_tokens(s, *arrays):
        for a in arrays:
            for origin in range(toks):
                ref = dst_of(s, a, origin)
                pltpu.make_async_copy(ref, ref, recv_sem.at[s, a, origin]).wait()

    for a in (K, V, Q):
        own(0, a).start()
        own(2, a).start()

    def widen(s):
        rate = rate_ref[s, 0].astype(F32)
        for h in range(toks):
            wide = jnp.broadcast_to(rate[h:h + 1], (rate_wide.shape[3], part))
            rate_wide[s, h] = wide.T.astype(BF)

    widen(0)
    own(0, RATE).start()

    barrier = pltpu.get_barrier_semaphore()
    greet = [(b, dest) for dest in others] + [(pair, tok) for tok in range(toks)]
    greet += [(after2, t), (before2, t)]
    for device in greet:
        pl.semaphore_signal(barrier, inc=1, device_id=device, device_id_type=MESH)
    pl.semaphore_wait(barrier, len(greet))

    for a in (K, RATE, V):
        exchange(0, a)
    widen(1)
    for a in (K, RATE, V):
        for slot, dest in enumerate(side):
            send(1, a, pair, dest, 2 + slot)
    widen(2)
    own(2, RATE).start()

    def each(count):
        return pl.loop(0, count // rows_of)

    def chunk(i):
        return pl.ds(pl.multiple_of(i * rows_of, rows_of), rows_of)

    for m in range(3):
        load_w(m).wait()

        @each(width)
        def _(i):
            rows = chunk(i)
            whi[0, m, rows], wlo[0, m, rows] = split(wf[m, rows])

    def forward(s, bank):
        @each(length)
        def _(i):
            rows = chunk(i)
            k = held[K, s, rows]
            rate = eta[s, rows].astype(F32)
            rate = jnp.concatenate([rate] * (width // rate.shape[1]), axis=1)
            hidden = mm(k, whi[bank, 0]) + mm(k, wlo[bank, 0])
            gated = mm(k, whi[bank, 1]) + mm(k, wlo[bank, 1])
            gate_sig = jax.nn.sigmoid(hidden)
            active = rate * (hidden * gate_sig)
            abuf[0, rows], abuf[1, rows] = split(active * gated)
            fbuf[0, rows] = rate * gated * gate_sig * (1.0 + hidden * (1.0 - gate_sig))
            fbuf[1, rows] = active

    def backward(s, bank):
        @each(length)
        def _(i):
            rows = chunk(i)
            v = held[V, s, rows]
            over = ((1,), (1,))
            back = mm(v, whi[bank, 2], over) + mm(v, wlo[bank, 2], over)
            xbuf[0, rows], xbuf[1, rows] = split(back * fbuf[0, rows])
            xbuf[2, rows], xbuf[3, rows] = split(back * fbuf[1, rows])

    def update(s, m, bank):
        @each(width)
        def _(i):
            rows = chunk(i)
            over = ((0,), (0,))
            if m == 2:
                v = held[V, s]
                grad = mm(abuf[0, :, rows], v, over) + mm(abuf[1, :, rows], v, over)
            else:
                k = held[K, s, :, rows]
                grad = mm(k, xbuf[2 * m], over) + mm(k, xbuf[2 * m + 1], over)
            old = wf[m, rows]
            new = old + grad
            rescale = jnp.sqrt((jnp.mean(old * old, axis=1, keepdims=True) + epsilon)
                               / (jnp.mean(new * new, axis=1, keepdims=True) + epsilon))
            new = new * rescale
            wf[m, rows] = new
            whi[bank, m, rows], wlo[bank, m, rows] = split(new)

    def hand_on(m):
        return pltpu.make_async_remote_copy(
            src_ref=wsend.at[m], dst_ref=wrecv.at[m], send_sem=wsend_sem.at[m],
            recv_sem=wrecv_sem.at[m], device_id=(after2, t), device_id_type=MESH)

    def give(m):
        @each(width)
        def _(i):
            rows = chunk(i)
            wsend[m, rows] = encode(wf[m, rows] * scale)

        hand_on(m).start()

    def take(m, bank):
        hand_on(m).wait_recv()

        @each(width)
        def _(i):
            rows = chunk(i)
            fresh = decode(wrecv[m, rows]) * (1.0 / scale)
            wf[m, rows] = fresh
            whi[bank, m, rows], wlo[bank, m, rows] = split(fresh)

    def out_at(s, origin):
        return out_ref.at[s, 0, :, pl.ds(pl.multiple_of(origin * width, width), width)]

    def out_part(s, dest):
        return obuf.at[s, pl.ds(pl.multiple_of(dest * part, part), part)]

    def out_copy(s, block, dest, slot):
        return pltpu.make_async_remote_copy(
            src_ref=out_part(s, dest), dst_ref=out_at(s, t),
            send_sem=osend_sem.at[s, slot], recv_sem=orecv_sem.at[s, t],
            device_id=(block, dest), device_id_type=MESH)

    def apply(s, bank):
        wait_tokens(s, Q)
        home = s != 1
        block = b if home else pair
        for turn, dests in enumerate((far, side)):
            rows = pl.ds(pl.multiple_of(dests[0] * part, 2 * part), 2 * part)
            q = held[Q, s, rows]
            hidden = mm(q, whi[bank, 0]) + mm(q, wlo[bank, 0])
            gated = mm(q, whi[bank, 1]) + mm(q, wlo[bank, 1])
            hi, lo = split(jax.nn.silu(hidden) * gated)
            result = mm(hi, whi[bank, 2]) + (mm(lo, whi[bank, 2]) + mm(hi, wlo[bank, 2]))
            obuf[s, rows] = result.astype(BF)
            if turn and home:
                dests = [mate]
                pltpu.make_async_copy(out_part(s, t), out_at(s, t), orecv_sem.at[s, t]).start()
            for slot, dest in enumerate(dests):
                out_copy(s, block, dest, 2 * turn + slot).start()

    def wait_out_sent(s):
        home = s != 1
        block = b if home else pair
        for slot, dest in enumerate(others if home else far + side):
            out_copy(s, block, dest, slot).wait_send()

    wait_tokens(0, K, RATE)
    for a in (K, RATE):
        for slot, dest in enumerate(far):
            send(1, a, pair, dest, slot)
    forward(0, 0)
    wait_tokens(0, V)
    for slot, dest in enumerate(far):
        send(1, V, pair, dest, slot)
    backward(0, 0)
    for m in range(3):
        update(0, m, 1)

        @pl.when(odd == 1)
        def _():
            give(m)

    def send_rest():
        exchange(0, Q)
        for slot, dest in enumerate(far + side):
            send(1, Q, pair, dest, slot)
        for a in (K, RATE, V, Q):
            exchange(2, a)

    @pl.when(odd == 1)
    def _():
        wait_tokens(1, K, RATE, V)
        send_rest()

    @pl.when(odd == 0)
    def _():
        wait_tokens(1, K, RATE)
        forward(1, 1)
        wait_tokens(1, V)
        send_rest()
        backward(1, 1)
        for m in range(3):
            update(1, m, 3)
            give(m)

    apply(0, 1)

    @pl.when(odd == 0)
    def _():
        apply(1, 3)
        take(0, 2)
        take(1, 2)
        wait_tokens(2, K, RATE)
        forward(2, 2)
        take(2, 2)
        wait_tokens(2, V)
        backward(2, 2)

    @pl.when(odd == 1)
    def _():
        take(0, 2)
        take(1, 2)
        forward(1, 2)
        take(2, 2)
        backward(1, 2)
        for m in range(3):
            update(1, m, 3)
        apply(1, 3)
        wait_tokens(2, K, RATE)
        forward(2, 3)
        wait_tokens(2, V)
        backward(2, 3)

    for m in range(3):
        update(2, m, 0)
        pltpu.make_async_copy(wf.at[m], fast_out_ref.at[0, 0, m], wload_sem.at[m]).start()
    apply(2, 0)

    for s in range(steps):
        for origin in range(toks):
            ref = out_at(s, origin)
            pltpu.make_async_copy(ref, ref, orecv_sem.at[s, origin]).wait()
        wait_out_sent(s)
    for m in range(3):
        pltpu.make_async_copy(wf.at[m], fast_out_ref.at[0, 0, m], wload_sem.at[m]).wait()
        hand_on(m).wait_send()
    for a in range(4):
        for s in (0, 2):
            for slot, dest in enumerate(others):
                token_copy(s, a, b, dest, slot).wait_send()
        for slot, dest in enumerate(far + side):
            token_copy(1, a, pair, dest, slot).wait_send()


def local(fast_in, queries, keys, values, rates):
    blocks, toks = lax.axis_size("block"), lax.axis_size("tok")
    steps, _, part, _ = queries.shape
    width = fast_in.shape[-1]
    length = part * toks
    scale = 2.0 ** math.floor(math.log2(2.0 ** 15.8 / (0.2501 * math.sqrt(width))))
    anywhere = pl.BlockSpec(memory_space=pl.ANY)
    vmem, dma = pltpu.VMEM, pltpu.SemaphoreType.DMA
    lanes = 128
    return pl.pallas_call(
        functools.partial(kernel, blocks, toks, scale),
        out_shape=(jax.ShapeDtypeStruct(queries.shape, queries.dtype),
                   jax.ShapeDtypeStruct(fast_in.shape, fast_in.dtype)),
        in_specs=[anywhere] * 4 + [pl.BlockSpec(memory_space=pltpu.VMEM)],
        out_specs=(anywhere, anywhere),
        scratch_shapes=[
            vmem((3, steps, length, width), BF),
            vmem((steps, toks, part, lanes), BF),
            vmem((3, width, width), F32),
            vmem((4, 3, width, width), BF),
            vmem((4, 3, width, width), BF),
            vmem((3, width, width), BF),
            vmem((3, width, width), BF),
            vmem((2, length, width), BF),
            vmem((2, length, width), F32),
            vmem((4, length, width), BF),
            vmem((steps, length, width), BF),
            vmem((steps, length, lanes), BF),
            dma((steps, 4, toks)), dma((steps, 4, toks)),
            dma((3,)), dma((3,)), dma((3,)),
            dma((steps, toks)), dma((steps, toks)),
        ],
        compiler_params=pltpu.CompilerParams(
            collective_id=0, has_side_effects=True, vmem_limit_bytes=60 * 2**20),
        cost_estimate=pl.CostEstimate(
            flops=57 * 2 * length * width * width, bytes_accessed=2**24, transcendentals=0),
    )(fast_in, queries, keys, values, jnp.swapaxes(rates, 2, 3))


def solution(mesh):
    tokens = P(None, "block", "tok", None)
    weights = P("block", "tok", None, None, None)
    return jax.shard_map(
        local, mesh=mesh, in_specs=(weights, tokens, tokens, tokens, tokens),
        out_specs=(tokens, weights), check_vma=False)
```
